32 devices in a mesh: dp: 16 (over z, y, core), factor: 2 (over x).
Axes of the slice: x: 2, y: 2, z: 4, core: 2. Of those that a mesh axis runs over, the one named last changes fastest.
Arguments:
- grad_out: bfloat16 [16, 128, 14336], P('dp', None, 'factor'), may hold values from -6 to 6
- act_in: bfloat16 [16, 128, 4096], P('dp', None, 'factor'), may hold values from -6 to 6
- basis_out: bfloat16 [14336, 14336], P('factor', 'dp'), may hold values from -0.046875 to 0.046875
- basis_in: bfloat16 [4096, 4096], P('factor', 'dp'), may hold values from -0.09375 to 0.09375
- eigen_vals: bfloat16 [14336, 4096], P('dp'), may hold values from 0.25 to 4
- query_out: bfloat16 [16, 8, 14336], P(None, None, 'factor'), may hold values from -0.01171875 to 0.01171875
- query_in: bfloat16 [16, 8, 4096], P(None, None, 'factor'), may hold values from -0.01171875 to 0.01171875
Outputs:
- scores: float32 [16, 16], P('factor')
The draws below stay inside these ranges and needn't reach their ends.
All inputs are finite; a program needn't handle non-finite values.
Results may differ from the reference program's by a relative error of at most 0.023.
Values may be sent and summed in bfloat16 or wider, within the bound.
A program may use at most 128 MiB of HBM per device.

```python
import math
import jax
import jax.numpy as jnp
from jax import lax

D = 4096
FF = 14336
RANK = 8
TOKENS = 128
QUERIES = 16
SEQS = 16
N_FACTOR = 2


def block_scale(own_key, extent, shards, smallest, high):
    factor_of, own = 1.0, jax.random.fold_in(own_key, 6)
    for dim, parts in shards:
        heights = jnp.exp(jax.random.uniform(jax.random.fold_in(own, dim), (parts,), jnp.float32, smallest / len(shards), high / len(shards)))
        factor_of = factor_of * jnp.repeat(heights, extent[dim] // parts).reshape([-1 if axis == dim else 1 for axis in range(len(extent))])
    return factor_of


def normal_values(stream_key, dims, scale, most, pieces=(), dtype=jnp.bfloat16):
    array = scale * jax.random.normal(stream_key, dims, jnp.float32)
    if pieces:
        array = array * block_scale(stream_key, dims, pieces, -0.22, 0.18)
    return jnp.clip(array, -most, most).astype(dtype)


def setup_inputs(seed: int = 0) -> dict:
    seeds = jax.random.split(jax.random.key(seed), 8)
    return {
        "grad_out": normal_values(seeds[0], (SEQS, TOKENS, FF), 1.0, 6.0, ((0, 16), (2, 2))),
        "act_in": normal_values(seeds[1], (SEQS, TOKENS, D), 1.0, 6.0, ((0, 16), (2, 2))),
        "basis_out": normal_values(seeds[2], (FF, FF), FF ** -0.5, 0.046875, ((0, 2), (1, 16))),
        "basis_in": normal_values(seeds[3], (D, D), D ** -0.5, 0.09375, ((0, 2), (1, 16))),
        "eigen_vals": jnp.clip(jnp.exp(math.log(4.0) - 2.7725887 * jax.random.uniform(seeds[4], (FF, D), jnp.float32) ** block_scale(seeds[4], (FF, D), ((0, 16),), -0.2, 0.2)), 0.25, 4.0).astype(jnp.bfloat16),
        "query_out": normal_values(seeds[5], (QUERIES, RANK, FF), (FF * 16) ** -0.5, 0.01171875, ((2, 2),)),
        "query_in": normal_values(seeds[6], (QUERIES, RANK, D), (D * 64) ** -0.5, 0.01171875, ((2, 2),)),
    }


def rotate_blocks(data, basis, blocks):
    width = data.shape[1] // blocks
    data_blocks = data.reshape(data.shape[0], blocks, width).transpose(1, 0, 2)
    basis_blocks = basis.reshape(blocks, width, basis.shape[1])

    def add_block(total, operands):
        product = jnp.dot(operands[0], operands[1], preferred_element_type=jnp.float32)
        rounded = lax.optimization_barrier(product.astype(jnp.bfloat16))
        return total + rounded.astype(jnp.float32), None

    start_total = jnp.zeros((data.shape[0], basis.shape[1]), jnp.float32)
    total, _ = lax.scan(add_block, start_total, (data_blocks, basis_blocks))
    return total.astype(jnp.bfloat16)


def reference(grad_out, act_in, basis_out, basis_in, eigen_vals, query_out, query_in):
    grad_rot = rotate_blocks(grad_out.reshape(-1, FF), basis_out, N_FACTOR).reshape(SEQS, TOKENS, FF)
    act_rot = rotate_blocks(act_in.reshape(-1, D), basis_in, N_FACTOR).reshape(SEQS, TOKENS, D)
    query_rot = jnp.einsum("qrk,ki->qri", query_out.astype(jnp.float32), basis_out.astype(jnp.float32))
    value_rot = jnp.einsum("qrk,kj->qrj", query_in.astype(jnp.float32), basis_in.astype(jnp.float32)).astype(jnp.bfloat16)
    value_mat = value_rot.reshape(QUERIES * RANK, D)
    eigen_float = eigen_vals.astype(jnp.float32)

    def per_sequence(operands):
        contracted = lax.dot_general(operands[0], operands[1], (((0,), (0,)), ((), ())), preferred_element_type=jnp.float32)
        scaled = (contracted / eigen_float).astype(jnp.bfloat16)
        weighted = lax.dot_general(scaled, value_mat, (((1,), (1,)), ((), ())), preferred_element_type=jnp.float32)
        weighted = weighted.reshape(FF, QUERIES, RANK)
        return jnp.einsum("iqr,qri->q", weighted, query_rot)

    return lax.map(per_sequence, (grad_rot, act_rot))
```

```python
import functools

import jax
import jax.numpy as jnp
from jax import lax
from jax.experimental import pallas as pl
from jax.experimental.pallas import tpu as pltpu
from jax.sharding import PartitionSpec as P

F32 = jnp.float32
BF16 = jnp.bfloat16
MESH = pl.DeviceIdType.MESH
NA = 4
CHUNKS = 2


class Gather:
    def __init__(self, place, nb, own, buf, chunks, sems, wide):
        self.a, self.b, self.c = place
        self.nb, self.own, self.buf, self.chunks, self.wide = nb, own, buf, chunks, wide
        self.recv, self.up, self.down, self.across, self.core = sems
        self.sends = []

    def block(self, a, b, c):
        return (a * self.nb + b) * 2 + c

    def lane(self, m):
        return lax.rem(self.b + m, self.nb)

    def turn(self, n):
        if n == 0:
            return self.a
        if n == 1:
            return self.a + 1 - 2 * lax.rem(self.a, 2)
        if n == 2:
            return lax.rem(self.a + 2, 4)
        return 3 - self.a

    def send(self, src, block, h, sem, dev, conds):
        copy = pltpu.make_async_remote_copy(
            src_ref=src, dst_ref=self.buf(block, h), send_sem=sem, recv_sem=self.recv.at[block, h],
            device_id={"dp": dev}, device_id_type=MESH)
        self.sends.append((copy, conds))
        guard(conds, copy.start)

    def wait(self, block, h):
        other = self.block(self.a, self.b, 1 - self.c)
        pltpu.make_async_remote_copy(
            src_ref=self.buf(block, h), dst_ref=self.buf(block, h), send_sem=self.core.at[0, h],
            recv_sem=self.recv.at[block, h], device_id={"dp": other}, device_id_type=MESH).wait_recv()

    def step_up(self, src, block, h, m, k, conds):
        if k < NA - 1:
            self.send(src, block, h, self.up.at[m, k, h], self.block(self.a + 1, self.b, self.c), conds + [self.a < NA - 1])

    def step_down(self, src, block, h, m, k, conds):
        if k < NA - 1:
            self.send(src, block, h, self.down.at[m, k, h], self.block(self.a - 1, self.b, self.c), conds + [self.a > 0])

    def to_core(self, src, block, h, m, row, conds):
        self.send(src, block, h, self.core.at[m * NA + row, h], self.block(self.a, self.b, 1 - self.c), conds)

    def start(self):
        me = self.block(self.a, self.b, self.c)
        for h in range(self.chunks):
            src = self.own(h)
            self.step_up(src, me, h, 0, 0, [])
            self.step_down(src, me, h, 0, 0, [])
            for m in range(1, self.nb):
                self.send(src, me, h, self.across.at[m - 1, h], self.block(self.a, self.lane(m), self.c), [])
            self.to_core(src, me, h, 0, self.a, [])

    def line(self, k):
        for m in range(self.nb if self.wide else 1):
            for h in range(self.chunks):
                for sign in (-1, 1):
                    row = self.a + sign * (k + 1)
                    cond = row >= 0 if sign < 0 else row < NA
                    block = self.block(row, self.lane(m), self.c)
                    guard([cond], functools.partial(self.wait, block, h))
                    src = self.buf(block, h)
                    if sign < 0:
                        self.step_up(src, block, h, m, k + 1, [cond])
                    else:
                        self.step_down(src, block, h, m, k + 1, [cond])
                    self.to_core(src, block, h, m, row, [cond])

    def rows(self, n):
        block = self.block(self.turn(n), self.b, self.c)
        for h in range(self.chunks):
            for m in range(1, self.nb):
                self.send(self.buf(block, h), block, h, self.across.at[n * (self.nb - 1) + m - 1, h],
                          self.block(self.a, self.lane(m), self.c), [])

    def rows_wait(self, n):
        for m in range(1, self.nb):
            block = self.block(self.turn(n), self.lane(m), self.c)
            for h in range(self.chunks):
                self.wait(block, h)
                src = self.buf(block, h)
                if self.wide:
                    self.step_up(src, block, h, m, 0, [])
                    self.step_down(src, block, h, m, 0, [])
                self.to_core(src, block, h, m, self.turn(n), [])

    def core_wait(self, n, m):
        block = self.block(self.turn(n), self.lane(m), 1 - self.c)
        for h in range(self.chunks):
            self.wait(block, h)

    def finish(self):
        for copy, conds in self.sends:
            guard(conds, copy.wait_send)


def guard(conds, run):
    if not conds:
        run()
        return
    cond = conds[0]
    for more in conds[1:]:
        cond = jnp.logical_and(cond, more)

    @pl.when(cond)
    def _():
        run()


def tiles(width, most):
    start = 0
    while start < width:
        size = min(most, width - start)
        yield start, size
        start += size


def kernel(nb, nf, grad, act, bo, bi, ev, qo, qi, out, gbuf, abuf,
           bo_v, bi_v, slot, re, ev_v, rbuf, pbuf, precv, apart, arecv, gt, qsend, qrecv, vsend, vrecv, qrt, wacc, score, srecv,
           g_recv, g_up, g_down, g_across, g_core, a_recv, a_up, a_down, a_across, a_core,
           r_recv, r_up, r_down, r_across, r_core,
           load_sem, ev_sem, slot_sem, p_send, p_recv, ap_send, ap_recv, q_send, q_recv, v_send, v_recv, s_send, s_recv):
    d = lax.axis_index("dp")
    f = lax.axis_index("factor")
    nd = NA * nb * 2
    c = lax.rem(d, 2)
    b = lax.rem(d // 2, nb)
    a = d // (2 * nb)
    tok, ka = act.shape
    ni = bo.shape[1]
    nj = bi.shape[1]
    nq = qo.shape[0]
    own_n = nd // nf
    rows = tok // CHUNKS

    loads = [(bo, bo_v), (bi, bi_v), (qo, slot.at[0, pl.ds(0, nq)]), (qi, slot.at[1, pl.ds(0, nq), pl.ds(0, ka)])]
    loads = [pltpu.make_async_copy(s, t, load_sem.at[i]) for i, (s, t) in enumerate(loads)]
    for load in loads:
        load.start()

    barrier = pltpu.get_barrier_semaphore()
    peers = [{"dp": (a * nb + b) * 2 + 1 - c}]
    peers += [{"dp": (a * nb + lax.rem(b + m, nb)) * 2 + c} for m in range(1, nb)]
    peers += [{"dp": (lax.rem(a + m, NA) * nb + b) * 2 + c} for m in range(1, NA)]
    peers += [{"factor": lax.rem(f + m, nf)} for m in range(1, nf)]
    for peer in peers:
        pl.semaphore_signal(barrier, inc=1, device_id=peer, device_id_type=MESH)
    pl.semaphore_wait(barrier, len(peers))

    place = (a, b, c)
    A = Gather(place, nb, lambda h: act, lambda k, h: abuf.at[k], 1, (a_recv, a_up, a_down, a_across, a_core), False)
    G = Gather(place, nb, lambda h: grad.at[pl.ds(h * rows, rows)], lambda k, h: gbuf.at[k, pl.ds(h * rows, rows)], CHUNKS,
               (g_recv, g_up, g_down, g_across, g_core), False)
    R = Gather(place, nb, lambda h: rbuf.at[d], lambda k, h: rbuf.at[k], 1, (r_recv, r_up, r_down, r_across, r_core), True)
    A.start()
    G.start()

    def swap(src, dst, send, recv):
        copies = [pltpu.make_async_remote_copy(
            src_ref=src, dst_ref=dst.at[m - 1], send_sem=send.at[m - 1], recv_sem=recv.at[m - 1],
            device_id={"factor": lax.rem(f + m, nf)}, device_id_type=MESH) for m in range(1, nf)]
        for copy in copies:
            copy.start()
        return copies

    for load in loads:
        load.wait()
    for start, size in tiles(ni, 256):
        qsend[:, start:start + size] = jnp.dot(slot[0, :nq, :], bo_v[:, start:start + size], preferred_element_type=F32)
    vsend[...] = jnp.dot(slot[1, :nq, :ka], bi_v[...], preferred_element_type=F32)
    q_copies = swap(qsend, qrecv, q_send, q_recv)
    v_copies = swap(vsend, vrecv, v_send, v_recv)

    def ev_load(k, par):
        return pltpu.make_async_copy(ev.at[:, pl.ds(pl.multiple_of(k * nj, nj), nj)], ev_v.at[par], ev_sem.at[par])

    ev_load(0, 0).start()

    def ev_step(k, carry):
        par = lax.rem(k, 2)

        @pl.when(k + 1 < nd)
        def _():
            ev_load(k + 1, 1 - par).start()

        ev_load(k, par).wait()
        re[k] = 1.0 / ev_v[par].astype(F32)
        return carry

    lax.fori_loop(0, nd, ev_step, 0)

    A.line(0)
    A.rows(1)
    A.rows_wait(0)
    A.line(1)
    A.rows(2)
    A.rows_wait(1)
    A.line(2)
    A.rows(3)
    A.rows_wait(2)
    A.rows_wait(3)

    order = [(n, m) for n in range(NA) for m in range(nb)]

    def pair_of(n, m):
        return G.turn(n) * nb + G.lane(m)

    def slot_load(index, buf, own, width, par):
        n, m = order[index]
        p = pair_of(n, m)
        copies = []
        for e in range(2):
            core = c if e == 0 else 1 - c
            src = own if index == 0 and e == 0 else buf.at[2 * p + core]
            dst = slot.at[par, pl.ds(pl.multiple_of(core * tok, tok), tok)]
            if width is not None:
                dst = slot.at[par, pl.ds(pl.multiple_of(core * tok, tok), tok), pl.ds(0, width)]
            copies.append(pltpu.make_async_copy(src, dst, slot_sem.at[par, e]))
        return copies

    def part_copy(index, half, part, recv, send_sem, recv_sem):
        s = 2 * pair_of(*order[index]) + half
        owner = lax.rem(s, nf)
        q = lax.rem(f - owner + nf, nf) - 1
        q = jnp.maximum(q, 0)
        return owner, s // nf, pltpu.make_async_remote_copy(
            src_ref=part.at[index, pl.ds(half * tok, tok)], dst_ref=recv.at[q, s // nf],
            send_sem=send_sem.at[index, half], recv_sem=recv_sem.at[q, s // nf],
            device_id={"factor": owner}, device_id_type=MESH)

    def part_send(index, part, recv, send_sem, recv_sem):
        for half in range(2):
            owner, _, copy = part_copy(index, half, part, recv, send_sem, recv_sem)
            guard([owner != f], copy.start)

    def part_done(index, part, recv, send_sem, recv_sem):
        for half in range(2):
            owner, _, copy = part_copy(index, half, part, recv, send_sem, recv_sem)
            guard([owner != f], copy.wait_send)

    def part_sum(index, half, j, part, recv, recv_sem):
        total = part[index, half * tok:(half + 1) * tok, :].astype(F32)
        for q in range(nf - 1):
            pltpu.make_async_remote_copy(
                src_ref=recv.at[q, j], dst_ref=recv.at[q, j], send_sem=v_send.at[0], recv_sem=recv_sem.at[q, j],
                device_id={"factor": lax.rem(f + 1, nf)}, device_id_type=MESH).wait_recv()
            total += recv[q, j].astype(F32)
        return total

    for n, m in order:
        A.core_wait(n, m)
    now = slot_load(0, abuf, act, ka, 0)
    for copy in now:
        copy.start()
    for index in range(len(order)):
        par = index % 2
        later = []
        if index + 1 < len(order):
            later = slot_load(index + 1, abuf, act, ka, 1 - par)
            for copy in later:
                copy.start()
        for copy in now:
            copy.wait()
        apart[index] = jnp.dot(slot[par, :, :ka], bi_v[...], preferred_element_type=F32).astype(BF16)
        part_send(index, apart, arecv, ap_send, ap_recv)
        now = later

    for copy in q_copies + v_copies:
        copy.wait()
    qsum = qsend[...]
    vsum = vsend[...]
    for q in range(nf - 1):
        qsum += qrecv[q]
        vsum += vrecv[q]
    qrt[...] = qsum.T
    rbuf[d, own_n * tok:, :] = vsum.astype(BF16)

    G.line(0)
    G.rows(1)

    for index in range(len(order)):
        for half in range(2):
            s = 2 * pair_of(*order[index]) + half

            @pl.when(lax.rem(s, nf) == f)
            def _():
                j = s // nf
                total = part_sum(index, half, j, apart, arecv, ap_recv)
                rbuf[d, pl.ds(pl.multiple_of(j * tok, tok), tok), :] = total.astype(BF16)

    R.start()

    def rotate(par, index):
        def body(k, carry):
            cols = pl.ds(pl.multiple_of(k * 256, 128), 256)
            pbuf[index, :, cols] = jnp.dot(slot[par], bo_v[:, cols], preferred_element_type=F32).astype(BF16)
            return carry

        whole = ni // 256
        lax.fori_loop(0, whole, body, 0)
        if whole * 256 < ni:
            pbuf[index, :, whole * 256:] = jnp.dot(
                slot[par], bo_v[:, whole * 256:], preferred_element_type=F32).astype(BF16)

    def multiply(index):
        n, m = order[index]
        G.core_wait(n, m)
        par = index % 2
        copies = slot_load(index, gbuf, grad, None, par)
        for copy in copies:
            copy.start()
        for copy in copies:
            copy.wait()
        rotate(par, index)
        part_send(index, pbuf, precv, p_send, p_recv)

    def finalize(index):
        for half in range(2):
            s = 2 * pair_of(*order[index]) + half

            @pl.when(lax.rem(s, nf) == f)
            def _():
                j = s // nf
                total = part_sum(index, half, j, pbuf, precv, p_recv)
                gt[j] = total.astype(BF16).astype(F32).T.astype(BF16)

    def score_one(j):
        wacc[...] = jnp.zeros_like(wacc)

        def body(k, carry):
            part = rbuf[k, pl.ds(pl.multiple_of(j * tok, tok), tok), :]
            contracted = jnp.dot(gt[j], part, preferred_element_type=F32)
            scaled = (contracted * re[k]).astype(BF16)
            wacc[...] += lax.dot_general(scaled, rbuf[k, own_n * tok:, :], (((1,), (1,)), ((), ())),
                                         preferred_element_type=F32)
            return carry

        lax.fori_loop(0, nd, body, 0)
        score[0, pl.ds(j, 1), :] = jnp.sum(wacc[...] * qrt[...], axis=0, keepdims=True)

    def score_pairs(first, last):
        def body(index, carry):
            n = index // nb
            m = lax.rem(index, nb)
            row = jnp.where(n == 0, G.turn(0), jnp.where(n == 1, G.turn(1), jnp.where(n == 2, G.turn(2), G.turn(3))))
            p = row * nb + lax.rem(b + m, nb)

            def each(half, carry):
                s = 2 * p + half

                @pl.when(lax.rem(s, nf) == f)
                def _():
                    score_one(s // nf)

                return carry

            return lax.fori_loop(0, 2, each, carry)

        lax.fori_loop(first, last, body, 0)

    multiply(0)
    R.rows_wait(0)
    G.rows_wait(0)
    for m in range(1, nb):
        multiply(m)
    R.line(0)
    G.line(1)
    G.rows(2)
    R.line(1)
    multiply(nb)
    G.rows_wait(1)
    for m in range(1, nb):
        multiply(nb + m)
    R.line(2)
    for index in range(nb):
        finalize(index)
    for n, m in order:
        R.core_wait(n, m)
    G.line(2)
    G.rows(3)
    score_pairs(0, nb)
    multiply(2 * nb)
    G.rows_wait(2)
    for m in range(1, nb):
        multiply(2 * nb + m)
    for index in range(nb, 2 * nb + 1):
        finalize(index)
    score_pairs(nb, 2 * nb + 1)
    multiply(3 * nb)
    for index in range(2 * nb + 1, 3 * nb + 1):
        finalize(index)
    score_pairs(2 * nb + 1, 3 * nb + 1)
    G.rows_wait(3)
    for m in range(1, nb):
        multiply(3 * nb + m)
    for index in range(3 * nb + 1, 4 * nb):
        finalize(index)
    score_pairs(3 * nb + 1, 4 * nb)

    copies = []
    bits = nd.bit_length() - 1
    for k in range(bits):
        step = 1 << k
        peer = d + step * (1 - 2 * lax.rem(d // step, 2))
        copy = pltpu.make_async_remote_copy(
            src_ref=score.at[k], dst_ref=srecv.at[k], send_sem=s_send.at[k], recv_sem=s_recv.at[k],
            device_id={"dp": peer}, device_id_type=MESH)
        copy.start()
        copy.wait_recv()
        score[k + 1] = score[k] + srecv[k]
        copies.append(copy)
    for m in range(1, nf):
        copy = pltpu.make_async_remote_copy(
            src_ref=score.at[bits], dst_ref=srecv.at[bits + m - 1], send_sem=s_send.at[bits + m - 1],
            recv_sem=s_recv.at[bits + m - 1], device_id={"factor": lax.rem(f + m, nf)}, device_id_type=MESH)
        copy.start()
        copies.append(copy)
    out[f] = score[bits]
    for m in range(1, nf):
        copies[bits + m - 1].wait_recv()
        out[lax.rem(f - m + nf, nf)] = srecv[bits + m - 1]
    for copy in copies:
        copy.wait_send()
    A.finish()
    G.finish()
    R.finish()
    for index in range(len(order)):
        part_done(index, apart, arecv, ap_send, ap_recv)
        part_done(index, pbuf, precv, p_send, p_recv)


def shards(nd, nf, grad_out, act_in, basis_out, basis_in, eigen_vals, query_out, query_in):
    nb = nd // (2 * NA)
    tok, kg = grad_out.shape[1:]
    ka = act_in.shape[2]
    ni = basis_out.shape[1]
    nj = basis_in.shape[1]
    queries, rank = query_out.shape[:2]
    nq = queries * rank
    own_n = nd // nf
    pairs = nd // 2
    bits = nd.bit_length() - 1
    dma = pltpu.SemaphoreType.DMA

    def sems(chunks, lanes):
        return [dma((nd, chunks)), dma((lanes, NA - 1, chunks)), dma((lanes, NA - 1, chunks)),
                dma((NA * max(nb - 1, 1), chunks)), dma((NA * nb, chunks))]

    any_spec = pl.BlockSpec(memory_space=pl.ANY)
    scores, _, _ = pl.pallas_call(
        functools.partial(kernel, nb, nf),
        out_shape=(jax.ShapeDtypeStruct((nf, own_n, nq), F32), jax.ShapeDtypeStruct((nd, tok, kg), BF16),
                   jax.ShapeDtypeStruct((nd, tok, ka), BF16)),
        in_specs=[any_spec] * 7,
        out_specs=(pl.BlockSpec(memory_space=pltpu.VMEM), any_spec, any_spec),
        scratch_shapes=[
            pltpu.VMEM(basis_out.shape, BF16), pltpu.VMEM(basis_in.shape, BF16), pltpu.VMEM((2, 2 * tok, kg), BF16),
            pltpu.VMEM((nd, ni, nj), F32), pltpu.VMEM((2, ni, nj), BF16), pltpu.VMEM((nd, own_n * tok + nq, nj), BF16),
            pltpu.VMEM((pairs, 2 * tok, ni), BF16), pltpu.VMEM((nf - 1, own_n, tok, ni), BF16),
            pltpu.VMEM((pairs, 2 * tok, nj), BF16), pltpu.VMEM((nf - 1, own_n, tok, nj), BF16),
            pltpu.VMEM((own_n, ni, tok), BF16), pltpu.VMEM((nq, ni), F32), pltpu.VMEM((nf - 1, nq, ni), F32),
            pltpu.VMEM((nq, nj), F32), pltpu.VMEM((nf - 1, nq, nj), F32), pltpu.VMEM((ni, nq), F32),
            pltpu.VMEM((ni, nq), F32), pltpu.VMEM((bits + 1, own_n, nq), F32), pltpu.VMEM((bits + nf - 1, own_n, nq), F32),
            *sems(CHUNKS, 1), *sems(1, 1), *sems(1, nb),
            dma((4,)), dma((2,)), dma((2, 2)), dma((pairs, 2)), dma((nf - 1, own_n)), dma((pairs, 2)), dma((nf - 1, own_n)),
            dma((nf - 1,)), dma((nf - 1,)), dma((nf - 1,)), dma((nf - 1,)), dma((bits + nf - 1,)), dma((bits + nf - 1,)),
        ],
        compiler_params=pltpu.CompilerParams(
            collective_id=0, has_side_effects=True, vmem_limit_bytes=63 * 1024 * 1024),
    )(grad_out.reshape(tok, kg), act_in.reshape(tok, ka), basis_out, basis_in, eigen_vals,
      query_out.reshape(nq, kg), query_in.reshape(nq, ka))
    f = lax.axis_index("factor")
    scores = scores.reshape(nf, own_n, queries, rank).sum(-1)
    whole = scores.transpose(1, 0, 2).reshape(nd, queries)
    return lax.dynamic_slice_in_dim(whole, f * own_n, own_n, 0)


def solution(mesh):
    in_specs = (
        P("dp", None, "factor"),
        P("dp", None, "factor"),
        P("factor", "dp"),
        P("factor", "dp"),
        P("dp", None),
        P(None, None, "factor"),
        P(None, None, "factor"),
    )
    body = functools.partial(shards, mesh.shape["dp"], mesh.shape["factor"])
    return jax.shard_map(body, mesh=mesh, in_specs=in_specs, out_specs=P("factor", None), check_vma=False)
```
